32 devices in a mesh: sites: 2 (over x), blk: 16 (over z, y, core).
Axes of the slice: x: 2, y: 2, z: 4, core: 2. Of those that a mesh axis runs over, the one named last changes fastest.
Arguments:
- green: bfloat16 [4096, 2, 2, 256], P(('sites', 'blk')), parts along dimension 0, may hold values from -9 to 9
- slip: bfloat16 [2, 256, 8, 128], P(None, 'blk'), may hold values from 0.049804688 to 1
- onset_bin: int32 [2, 256, 128], P(None, 'blk'), may hold values from 0 to 3
- item_helper: int32 [2, 256, 1], P(None, 'blk'), may hold values from 0 to 15; in each aligned block of 16 rows (0 to 15, 16 to 31, ..., all dimensions but the last counted through in order) at most 2 rows name the same one
- item_rupture: int32 [2, 256], P(None, 'blk'), may hold values from 0 to 3
- base_shift: int32 [2, 64, 8], P(None, 'blk'), may hold values from 0 to 511
- rupture_rate: float32 [2, 64], P(None, 'blk'), may hold values from 0.00046875 to 1.5625, as said below
Outputs:
- seismograms: float32 [2, 128, 8, 2, 512], P(None, ('sites', 'blk')), parts along dimension 1
- site_log_power: float32 [4, 256], P('sites'), parts along dimension 0
The draws below stay inside these ranges and needn't reach their ends.
There are 2 independent parts, one for each index of `sites`. The reference program is written for one: setup_inputs(seed, part) draws one part's arguments, and reference() takes and returns one part's arrays. A program takes and returns all parts, laid end to end along the dimension named above; an argument that names none is the same for every part. Nothing has to cross between parts.
Inputs may be any that keep to these rules, and one draw needn't show every extreme that they name: `item_helper`: in each batch, the 16 segments of one device name no helper more than 2 times. `rupture_rate`: positive rates.
All inputs are finite; a program needn't handle non-finite values.
Results may differ from the reference program's by a relative error of at most 0.0015.
Values may be sent and summed in bfloat16 or wider, within the bound.
A program may use at most 128 MiB of HBM per device.

```python
import math
import jax
import jax.numpy as jnp
import numpy as np
from jax import lax

FREQS = 256
COMPS = 2
VARIATIONS = 8
ONSET_BINS = 4
BIN_LAG = 9
BATCHES = 2
CAPACITY = 2
SAMPLES = 512
SUB_HELPER = 128
SUBFAULTS_ALL = 2048
ITEM_DEV = 16
RUPT_DEV = 4
ITEMS = 256
RUPTURES = 64
N_BLK = 16


def draw_green(key, part):
    shape_all = (SUBFAULTS_ALL, COMPS, 2, FREQS)
    shared_key = jax.random.fold_in(key, 11)
    own_part = jax.random.truncated_normal(key, -4.0, 4.0, shape_all, jnp.float32)
    shared = 0.8 * jax.random.truncated_normal(shared_key, -2.0, 2.0, (1, COMPS, 2, FREQS), jnp.float32)
    values = own_part + shared
    return values.astype(jnp.bfloat16)


def draw_rupture_rate(key, part):
    owners = jnp.arange(RUPTURES, dtype=jnp.int32) // RUPT_DEV
    owners_all = RUPTURES // RUPT_DEV
    rising = 1.0 + 2.0 * owners.astype(jnp.float32) / max(owners_all - 1, 1)
    common = jnp.exp(jax.random.uniform(jax.random.fold_in(key, 7), (), jnp.float32, -0.7, 0.7))
    ratio_log = jax.random.uniform(jax.random.fold_in(key, 17), (), jnp.float32, math.log(2.0), math.log(4.0))
    upward = jax.random.bernoulli(jax.random.fold_in(key, 19))
    ratio = jnp.exp(jnp.where(upward, ratio_log, -ratio_log))
    levels = jnp.where(jnp.arange(BATCHES, dtype=jnp.int32) == 1, ratio, 1.0).astype(jnp.float32)
    factor = jnp.exp(jax.random.uniform(key, (BATCHES, RUPTURES), jnp.float32, math.log(0.3), math.log(3.0)))
    return (factor * levels[:, None] * common * rising[None, :] / RUPTURES).astype(jnp.float32)


def touch_ends(values, stream_key, least, top_value):
    place = [jax.random.randint(jax.random.fold_in(stream_key, axis), (), 0, length) for axis, length in enumerate(values.shape)]
    widest = values.shape.index(max(values.shape))
    next_to = place[:widest] + [(place[widest] + 1) % values.shape[widest]] + place[widest + 1:]
    return values.at[tuple(place)].set(least).at[tuple(next_to)].set(top_value)


def level_of(stream_key, extent, cuts, low, top_value):
    factor_of, own = 1.0, jax.random.fold_in(stream_key, 6)
    for dim, blocks in cuts:
        steps = jnp.exp(jax.random.uniform(jax.random.fold_in(own, dim), (blocks,), jnp.float32, low / len(cuts), top_value / len(cuts)))
        factor_of = factor_of * jnp.repeat(steps, extent[dim] // blocks).reshape([-1 if axis == dim else 1 for axis in range(len(extent))])
    return factor_of


def assign_block(key, own, number, rows, number_of, top, most, slope):
    order = jax.random.permutation(key, number_of)
    packed, ordinary = load_shares(number_of, rows * top, most, slope, True), load_shares(number_of, rows * top, most, slope, False)
    places = jnp.arange(number_of)

    def named(tallies, turn):
        used = int((tallies > 0).sum())
        fixed = max(1, used // 4)
        passed = fixed + (places - fixed + turn * (used - fixed)) % max(1, number_of - fixed)
        return jnp.zeros((number_of,), jnp.int32).at[order[jnp.where(places < fixed, places, passed)]].set(jnp.asarray(tallies, jnp.int32))

    tallies = jnp.where(number % 4 == 0, named(packed, number // 4), named(ordinary, number - number // 4 - 1))
    mixed = jax.random.permutation(jax.random.fold_in(own, 3), number_of)
    giver, taker = mixed[0:number_of // 2 * 2:2], mixed[1:number_of // 2 * 2:2]
    room = jnp.minimum(tallies[giver] - 1, most - tallies[taker]) // 2
    room = jnp.where((giver == order[0]) | (taker == order[0]) | (tallies[taker] == 0), 0, jnp.maximum(room, 0))
    passed = jax.random.randint(jax.random.fold_in(own, 4), (number_of // 2,), 0, 1 << 20) % (room + 1)
    tallies = tallies.at[giver].add(-passed).at[taker].add(passed)
    members = jnp.searchsorted(jnp.cumsum(tallies), jnp.arange(rows * top), side="right").astype(jnp.int32)
    grid = members.reshape(top, rows).T
    grid = grid[jax.random.permutation(jax.random.fold_in(own, 1), rows)]
    turn = jax.random.randint(jax.random.fold_in(own, 2), (rows, 1), 0, top)
    return jnp.take_along_axis(grid, (jnp.arange(top)[None, :] + turn) % top, axis=1)


def load_shares(count, total, most, slope, full):
    portions = [(1 << 20) // math.isqrt(standing ** slope) + 1 for standing in range(1, count + 1)]
    largest = most if full else min(most, max(-(-total // count), total * portions[0] // sum(portions)))
    least = 1 if total - largest >= count - 1 else 0
    given, surplus = [largest] + [least] * (count - 1), total - largest - least * (count - 1)
    while surplus > 0:
        movable = [i for i in range(1, count) if given[i] < largest] or [i for i in range(1, count) if given[i] < most]
        mass, left = sum([portions[i] for i in movable]), surplus
        for i in movable:
            more = min(most - given[i], max(1, left * portions[i] // mass), surplus)
            given[i] = given[i] + more
            surplus = surplus - more
    return np.array(given)


def setup_inputs(seed: int = 0, part: int = 0) -> dict:
    arg_keys = jax.random.split(jax.random.key(seed), 8)
    part_splits = jax.random.split(jax.random.fold_in(arg_keys[7], part), 8)
    green = draw_green(jax.random.fold_in(jax.random.fold_in(arg_keys[7], part), 71), part)
    slip = jnp.clip(jnp.exp(math.log(1.0) - 2.9996462 * jax.random.uniform(arg_keys[1], (BATCHES, ITEMS, VARIATIONS, SUB_HELPER), jnp.float32) ** level_of(arg_keys[1], (BATCHES, ITEMS, VARIATIONS, SUB_HELPER), ((1, 16),), -0.2, 0.2)), 0.049804688, 1.0).astype(jnp.bfloat16)
    onset_bin = touch_ends(jax.random.randint(arg_keys[2], (BATCHES, ITEMS, SUB_HELPER), 0, ONSET_BINS), jax.random.fold_in(arg_keys[2], 1), 0, ONSET_BINS - 1).astype(jnp.int32)
    item_helper_keys = jax.random.split(jax.random.fold_in(arg_keys[3], 1), BATCHES * ITEMS // ITEM_DEV)
    item_helper_turns = jax.random.permutation(jax.random.fold_in(arg_keys[3], 3), BATCHES * ITEMS // ITEM_DEV)
    item_helper = jax.vmap(lambda own, number: assign_block(jax.random.fold_in(arg_keys[3], 2), own, number, ITEM_DEV, N_BLK, 1, CAPACITY, 2))(item_helper_keys, item_helper_turns).reshape((BATCHES, ITEMS, 1))
    item_rupture = touch_ends(jax.random.randint(arg_keys[4], (BATCHES, ITEMS), 0, RUPT_DEV), jax.random.fold_in(arg_keys[4], 1), 0, RUPT_DEV - 1).astype(jnp.int32)
    base_shift = touch_ends(jax.random.randint(arg_keys[5], (BATCHES, RUPTURES, VARIATIONS), 0, SAMPLES), jax.random.fold_in(arg_keys[5], 1), 0, SAMPLES - 1).astype(jnp.int32)
    rupture_rate = draw_rupture_rate(jax.random.fold_in(arg_keys[7], 71), part)
    return {"green": green, "slip": slip, "onset_bin": onset_bin, "item_helper": item_helper, "item_rupture": item_rupture, "base_shift": base_shift, "rupture_rate": rupture_rate}


def phase_tables():
    frequency = jnp.arange(FREQS, dtype=jnp.int32)
    bins_all = jnp.arange(ONSET_BINS, dtype=jnp.int32)
    turns = (bins_all[:, None] * BIN_LAG * frequency[None, :]) % SAMPLES
    angles = (2.0 * math.pi / SAMPLES) * turns.astype(jnp.float32)
    return jnp.cos(angles), jnp.sin(angles)


def inverse_table():
    frequency = jnp.arange(FREQS, dtype=jnp.int32)
    sample = jnp.arange(SAMPLES, dtype=jnp.int32)
    angles = (2.0 * math.pi / SAMPLES) * ((frequency[:, None] * sample[None, :]) % SAMPLES).astype(jnp.float32)
    weight = jnp.where(frequency == 0, 1.0 / SAMPLES, 2.0 / SAMPLES).astype(jnp.float32)[:, None]
    return jnp.concatenate([weight * jnp.cos(angles), -weight * jnp.sin(angles)], axis=0)


def item_partial(green_rows, slip_rows, onset_rows, cosines, sines):
    binned = jnp.arange(ONSET_BINS, dtype=jnp.int32)[:, None, None] == onset_rows[None, None, :]
    masked = jnp.where(binned, slip_rows[None], jnp.zeros((), slip_rows.dtype))
    masked = masked.reshape(ONSET_BINS * VARIATIONS, SUB_HELPER)
    summed = jnp.dot(masked, green_rows, preferred_element_type=jnp.float32)
    summed = summed.reshape(ONSET_BINS, VARIATIONS, COMPS, 2, FREQS)
    cos_rows = cosines[:, None, None, :]
    sin_rows = sines[:, None, None, :]
    real_part = jnp.sum(cos_rows * summed[:, :, :, 0] + sin_rows * summed[:, :, :, 1], axis=0)
    imag_part = jnp.sum(cos_rows * summed[:, :, :, 1] - sin_rows * summed[:, :, :, 0], axis=0)
    return jnp.stack([real_part, imag_part], axis=2).astype(jnp.bfloat16)


def reference(green, slip, onset_bin, item_helper, item_rupture, base_shift, rupture_rate):
    cosines, sines = phase_tables()
    inverse = inverse_table()
    green_flat = green.reshape(SUBFAULTS_ALL, COMPS * 2 * FREQS)
    frequency = jnp.arange(FREQS, dtype=jnp.int32)
    outputs = []
    power_sum = jnp.zeros((COMPS, FREQS), jnp.float32)
    for batch_index in range(BATCHES):
        def one_item(item_index):
            helper = item_helper[batch_index, item_index, 0]
            start = (helper * SUB_HELPER).astype(jnp.int32)
            green_rows = lax.dynamic_slice_in_dim(green_flat, start, SUB_HELPER, 0)
            return item_partial(green_rows, slip[batch_index, item_index], onset_bin[batch_index, item_index], cosines, sines)

        partials = lax.map(one_item, jnp.arange(ITEMS, dtype=jnp.int32))
        owners = jnp.arange(ITEMS, dtype=jnp.int32) // ITEM_DEV
        rupture_ids = (owners * RUPT_DEV + item_rupture[batch_index]).astype(jnp.int32)
        spectrum = jax.ops.segment_sum(partials.astype(jnp.float32), rupture_ids, num_segments=RUPTURES)
        real_part = spectrum[:, :, :, 0]
        imag_part = spectrum[:, :, :, 1]
        turns = (base_shift[batch_index][:, :, None] * frequency[None, None, :]) % SAMPLES
        angles = (2.0 * math.pi / SAMPLES) * turns.astype(jnp.float32)
        cos_shift = jnp.cos(angles)[:, :, None, :]
        sin_shift = jnp.sin(angles)[:, :, None, :]
        shifted = jnp.stack([real_part * cos_shift + imag_part * sin_shift, imag_part * cos_shift - real_part * sin_shift], axis=3)
        seismo = jnp.dot(shifted.reshape(RUPTURES * VARIATIONS * COMPS, 2 * FREQS), inverse, precision=lax.Precision.HIGHEST)
        outputs.append(seismo.reshape(RUPTURES, VARIATIONS, COMPS, SAMPLES))
        energy = jnp.mean(real_part * real_part + imag_part * imag_part, axis=1)
        power_sum = power_sum + jnp.sum(rupture_rate[batch_index][:, None, None] * energy, axis=0)
    return jnp.stack(outputs, axis=0), jnp.log(power_sum)
```

```python
import functools
import math

import jax
import jax.numpy as jnp
import numpy as np
from jax import lax
from jax.experimental import pallas as pl
from jax.experimental.pallas import tpu as pltpu
from jax.sharding import PartitionSpec as P

BIN_LAG = 9
ONSET_BINS = 4
CAPACITY = 2
SAMPLES = 512
F32 = jnp.float32
BF16 = jnp.bfloat16


def phase_table(freqs, rows):
    turns = np.arange(ONSET_BINS)[:, None] * BIN_LAG * np.arange(freqs)[None, :] % SAMPLES
    angles = 2.0 * math.pi / SAMPLES * turns
    both = np.stack([np.cos(angles), np.sin(angles)])
    return np.repeat(both.reshape(2 * ONSET_BINS, freqs), rows, axis=0).astype(np.float32)


def inverse_table(freqs):
    frequency = np.arange(freqs)
    angles = 2.0 * math.pi / SAMPLES * (frequency[:, None] * np.arange(SAMPLES)[None, :] % SAMPLES)
    weight = np.where(frequency == 0, 1.0 / SAMPLES, 2.0 / SAMPLES)[:, None]
    return np.concatenate([weight * np.cos(angles), -weight * np.sin(angles)]).astype(np.float32)


def column(row):
    n = row.shape[1]
    diag = lax.broadcasted_iota(jnp.int32, (n, n), 0) == lax.broadcasted_iota(jnp.int32, (n, n), 1)
    return jnp.sum(jnp.where(diag, jnp.broadcast_to(row, (n, n)), 0.0), axis=1, keepdims=True)


def kernel(
    dims,
    green_ref,
    slip_ref,
    onset_ref,
    helper_ref,
    rupture_ref,
    shift_ref,
    rate_ref,
    phase_ref,
    inverse_ref,
    out_ref,
    power_ref,
    gat,
    rows_ref,
    acc,
    cos_ref,
    sin_ref,
    inv,
    pw,
    local_sem,
    ring_s,
    ring_r,
    sib_s,
    sib_r,
    pw_s,
    pw_r,
):
    devices, batches, items, variations, rupts, comps, freqs = dims
    subs = green_ref.shape[0]
    half_rows = subs // 2
    chips = devices // 2
    me = lax.axis_index("blk")
    core = me % 2
    chip = me // 2
    folded = chips % 2 == 0

    def chip_at(pos):
        if not folded:
            return pos
        back = pos // (chips // 2)
        return (1 - back) * 2 * pos + back * (2 * (chips - 1 - pos) + 1)

    if folded:
        odd = chip % 2
        q = (1 - odd) * (chip // 2) + odd * (chips - 1 - chip // 2)
    else:
        q = chip
    right = chip_at((q + 1) % chips) * 2 + core
    left = chip_at((q + chips - 1) % chips) * 2 + core
    sibling = chip * 2 + (1 - core)

    def chunk(side, j, shift, which):
        step = j // 2 + shift
        pos = (q + chips - step) % chips if side == 0 else (q + step) % chips
        half = j % 2 if side == 0 else 1 - j % 2
        return gat.at[pos * 2 + which, pl.ds(pl.multiple_of(half * half_rows, half_rows), half_rows)]

    def ring(side, j, shift):
        piece = chunk(side, j, shift, core)
        return pltpu.make_async_remote_copy(
            src_ref=piece,
            dst_ref=piece,
            send_sem=ring_s.at[side, j],
            recv_sem=ring_r.at[side, j],
            device_id={"blk": right if side == 0 else left},
            device_id_type=pl.DeviceIdType.MESH,
        )

    def sib(side, j, which):
        piece = chunk(side, j, 1, which)
        return pltpu.make_async_remote_copy(
            src_ref=piece,
            dst_ref=piece,
            send_sem=sib_s.at[side, j],
            recv_sem=sib_r.at[side, j],
            device_id={"blk": sibling},
            device_id_type=pl.DeviceIdType.MESH,
        )

    def sib_own(half, which):
        piece = gat.at[q * 2 + which, pl.ds(half * half_rows, half_rows)]
        return pltpu.make_async_remote_copy(
            src_ref=piece,
            dst_ref=piece,
            send_sem=sib_s.at[half, chips - 1],
            recv_sem=sib_r.at[half, chips - 1],
            device_id={"blk": sibling},
            device_id_type=pl.DeviceIdType.MESH,
        )

    own = pltpu.make_async_copy(green_ref, gat.at[q * 2 + core], local_sem.at[0])
    own.start()
    table = pltpu.make_async_copy(inverse_ref, inv, local_sem.at[1])
    table.start()
    barrier = pltpu.get_barrier_semaphore()

    @pl.loop(1, devices)
    def _(o):
        pl.semaphore_signal(
            barrier, inc=1, device_id={"blk": (me + o) % devices}, device_id_type=pl.DeviceIdType.MESH
        )

    pl.semaphore_wait(barrier, devices - 1)
    own.wait()
    for j in range(min(2, chips - 1)):
        for side in range(2):
            ring(side, j, 0).start()
    for half in range(2):
        sib_own(half, core).start()

    total = batches * items
    lanes = total * variations
    slots = batches * CAPACITY
    group = ONSET_BINS * variations
    cols = subs
    helper_col = jnp.concatenate([column(helper_ref[b].astype(F32)) for b in range(batches)], axis=0)
    rupture_col = jnp.concatenate(
        [column(rupture_ref[b : b + 1, :].astype(F32)) for b in range(batches)], axis=0
    )
    lane = lax.broadcasted_iota(jnp.int32, (total, lanes), 1)
    lane_item = lane // variations
    item = lax.broadcasted_iota(jnp.int32, (total, lanes), 0)
    helper_lane = jnp.sum(jnp.where(lane_item == item, helper_col, 0.0), axis=0, keepdims=True)
    earlier = jnp.logical_and(item < lane_item, item // items == lane_item // items)
    same = jnp.logical_and(helper_col == helper_lane, earlier)
    rank = jnp.sum(jnp.where(same, 1.0, 0.0), axis=0, keepdims=True)
    lane1 = lax.broadcasted_iota(jnp.int32, (1, lanes), 1)
    batch1 = lane1 // (variations * items)
    key = (helper_lane.astype(jnp.int32) * slots + batch1 * CAPACITY + rank.astype(jnp.int32)) * variations
    key = key + lane1 % variations
    target = lax.broadcasted_iota(jnp.int32, (slots * group, lanes), 0)
    target = target // group * variations + target % variations
    slip_rows = slip_ref[...].astype(F32).reshape(lanes, subs)
    rows_ref[:, :cols] = slip_rows.astype(BF16)
    onset_rows = onset_ref[...].astype(F32).reshape(total, 1, subs)
    onset_rows = jnp.broadcast_to(onset_rows, (total, variations, subs)).reshape(lanes, subs)
    rows_ref[:, cols : 2 * cols] = onset_rows.astype(BF16)
    rupture_rows = jnp.broadcast_to(rupture_col, (total, 128)).reshape(total, 1, 128)
    rupture_rows = jnp.broadcast_to(rupture_rows, (total, variations, 128)).reshape(lanes, 128)
    rows_ref[:, 2 * cols :] = rupture_rows.astype(BF16)
    row_bin = lax.broadcasted_iota(jnp.int32, (slots * group, subs), 0) % group // variations
    row_bin = row_bin.astype(F32)
    acc[...] = jnp.zeros_like(acc)

    def compute(pos, which):
        h = chip_at(pos) * 2 + which
        pick = jnp.where(key - h * (slots * variations) == target, 1.0, 0.0).astype(BF16)
        picked = jnp.dot(pick, rows_ref[...], preferred_element_type=F32)
        masked = jnp.where(picked[:, cols : 2 * cols] == row_bin, picked[:, :cols], 0.0).astype(BF16)
        rupture = picked[:, 2 * cols :]
        for c in range(comps):
            lo = c * 2 * freqs
            summed = jnp.dot(
                masked, gat[pos * 2 + which, :, lo : lo + 2 * freqs], preferred_element_type=F32
            )
            for slot in range(slots):
                real_part = summed[slot * group : slot * group + variations, :freqs]
                imag_part = summed[slot * group : slot * group + variations, freqs:]
                real_sum, imag_sum = real_part, imag_part
                for k in range(1, ONSET_BINS):
                    at = slot * group + k * variations
                    real_part = summed[at : at + variations, :freqs]
                    imag_part = summed[at : at + variations, freqs:]
                    cos_k = phase_ref[k * variations : (k + 1) * variations, :]
                    s = (ONSET_BINS + k) * variations
                    sin_k = phase_ref[s : s + variations, :]
                    real_sum = real_sum + (cos_k * real_part + sin_k * imag_part)
                    imag_sum = imag_sum + (cos_k * imag_part - sin_k * real_part)
                both = jnp.concatenate([real_sum, imag_sum], axis=1).astype(BF16).astype(F32)
                named = rupture[slot * group : slot * group + variations, :]
                named = jnp.concatenate([named] * (2 * freqs // 128), axis=1)
                b = slot // CAPACITY
                for r in range(rupts):
                    base = (b * rupts + r) * variations
                    acc[base : base + variations, lo : lo + 2 * freqs] += jnp.where(
                        named == float(r), both, 0.0
                    )

    def arrive(j):
        for side in range(2):
            ring(side, j, 1).wait_recv()

            @pl.when(j + 2 <= chips - 2)
            def _():
                ring(side, j + 2, 0).start()

            sib(side, j, core).start()

    def sib_wait(j):
        for side in range(2):
            sib(side, j, 1 - core).wait_recv()

    def several(d, count):
        @pl.loop(0, count)
        def _(t):
            step = d - t // 2
            other = t // 2
            pos = (q + chips + (2 * (t % 2) - 1) * step) % chips
            compute(pos, core + other - 2 * core * other)

    frequency = lax.broadcasted_iota(jnp.int32, (variations, freqs), 1)
    for b in range(batches):
        for r in range(rupts):
            shift = column(shift_ref[b, r : r + 1, :].astype(F32)).astype(jnp.int32)
            turns = shift * frequency % SAMPLES
            angles = 2.0 * math.pi / SAMPLES * turns.astype(F32)
            base = (b * rupts + r) * variations
            cos_ref[base : base + variations, :] = jnp.cos(angles)
            sin_ref[base : base + variations, :] = jnp.sin(angles)

    compute(q, core)
    most = (chips - 1) // 2
    arrive(0)
    arrive(1)
    for half in range(2):
        sib_own(half, 1 - core).wait_recv()
    several(1, 3)

    @pl.loop(2, most + 1)
    def _(d):
        arrive(2 * d - 2)
        arrive(2 * d - 1)
        sib_wait(2 * d - 4)
        sib_wait(2 * d - 3)
        several(d, 4)

    if folded:
        arrive(chips - 2)
    sib_wait(2 * most - 2)
    sib_wait(2 * most - 1)
    if folded:
        compute((q + chips // 2) % chips, core)
    compute((q + chips - most) % chips, 1 - core)
    compute((q + most) % chips, 1 - core)
    if folded:
        sib_wait(chips - 2)
        compute((q + chips // 2) % chips, 1 - core)

    for c in range(comps):
        lo = c * 2 * freqs
        energy = jnp.zeros((variations, freqs), F32)
        for b in range(batches):
            for r in range(rupts):
                base = (b * rupts + r) * variations
                real_part = acc[base : base + variations, lo : lo + freqs]
                imag_part = acc[base : base + variations, lo + freqs : lo + 2 * freqs]
                square = real_part * real_part + imag_part * imag_part
                energy = energy + rate_ref[b : b + 1, r : r + 1] * square
        pw[me, c : c + 1, :] = jnp.sum(energy, axis=0, keepdims=True) * (1.0 / variations)

    def power_copy(o):
        return pltpu.make_async_remote_copy(
            src_ref=pw.at[me],
            dst_ref=pw.at[me],
            send_sem=pw_s.at[o],
            recv_sem=pw_r.at[o],
            device_id={"blk": (me + o) % devices},
            device_id_type=pl.DeviceIdType.MESH,
        )

    def power_arrival(o):
        slot = pw.at[(me + devices - o) % devices]
        return pltpu.make_async_remote_copy(
            src_ref=slot,
            dst_ref=slot,
            send_sem=pw_s.at[o],
            recv_sem=pw_r.at[o],
            device_id={"blk": (me + o) % devices},
            device_id_type=pl.DeviceIdType.MESH,
        )

    @pl.loop(1, devices)
    def _(o):
        power_copy(o).start()

    table.wait()
    cos_shift = cos_ref[...]
    sin_shift = sin_ref[...]
    for c in range(comps):
        lo = c * 2 * freqs
        real_part = acc[:, lo : lo + freqs]
        imag_part = acc[:, lo + freqs : lo + 2 * freqs]
        shifted = jnp.concatenate(
            [
                real_part * cos_shift + imag_part * sin_shift,
                imag_part * cos_shift - real_part * sin_shift,
            ],
            axis=1,
        )
        out_ref[:, c * SAMPLES : (c + 1) * SAMPLES] = jnp.dot(
            shifted, inv[...], precision=lax.Precision.HIGHEST, preferred_element_type=F32
        )

    @pl.loop(1, devices)
    def _(o):
        power_arrival(o).wait_recv()

    power_ref[...] = jnp.log(jnp.sum(pw[...], axis=0))

    @pl.loop(1, devices)
    def _(o):
        power_copy(o).wait_send()

    @pl.loop(0, chips - 1)
    def _(j):
        for side in range(2):
            ring(side, j, 0).wait_send()
            sib(side, j, core).wait_send()

    for half in range(2):
        sib_own(half, core).wait_send()


def local(green, slip, onset_bin, item_helper, item_rupture, base_shift, rupture_rate):
    devices = lax.axis_size("blk")
    subs, comps, _, freqs = green.shape
    batches, items, variations, _ = slip.shape
    rupts = base_shift.shape[1]
    width = comps * 2 * freqs
    rows = batches * rupts * variations
    chips = devices // 2
    dims = (devices, batches, items, variations, rupts, comps, freqs)
    gathered = devices * subs * width * 2
    vmem = pl.BlockSpec(memory_space=pltpu.VMEM)
    anywhere = pl.BlockSpec(memory_space=pl.ANY)
    seismo, power = pl.pallas_call(
        functools.partial(kernel, dims),
        out_shape=(
            jax.ShapeDtypeStruct((rows, comps * SAMPLES), F32),
            jax.ShapeDtypeStruct((comps, freqs), F32),
        ),
        in_specs=[anywhere, vmem, vmem, vmem, vmem, vmem, vmem, vmem, anywhere],
        out_specs=(vmem, vmem),
        scratch_shapes=[
            pltpu.VMEM((devices, subs, width), BF16),
            pltpu.VMEM((batches * items * variations, 2 * subs + 128), BF16),
            pltpu.VMEM((rows, width), F32),
            pltpu.VMEM((rows, freqs), F32),
            pltpu.VMEM((rows, freqs), F32),
            pltpu.VMEM((2 * freqs, SAMPLES), F32),
            pltpu.VMEM((devices, comps, freqs), F32),
            pltpu.SemaphoreType.DMA((2,)),
            pltpu.SemaphoreType.DMA((2, chips)),
            pltpu.SemaphoreType.DMA((2, chips)),
            pltpu.SemaphoreType.DMA((2, chips)),
            pltpu.SemaphoreType.DMA((2, chips)),
            pltpu.SemaphoreType.DMA((devices,)),
            pltpu.SemaphoreType.DMA((devices,)),
        ],
        compiler_params=pltpu.CompilerParams(
            collective_id=0, has_side_effects=True, vmem_limit_bytes=min(60, 20 + (gathered >> 20)) << 20
        ),
    )(
        green.reshape(subs, width),
        slip,
        onset_bin,
        item_helper.reshape(batches, 1, items),
        item_rupture,
        base_shift,
        rupture_rate,
        jnp.asarray(phase_table(freqs, variations)),
        jnp.asarray(inverse_table(freqs)),
    )
    return seismo.reshape(batches, rupts, variations, comps, SAMPLES), power


def solution(mesh):
    placed = (
        P(("sites", "blk"), None, None, None),
        P(None, "blk", None, None),
        P(None, "blk", None),
        P(None, "blk", None),
        P(None, "blk"),
        P(None, "blk", None),
        P(None, "blk"),
    )
    return jax.shard_map(
        local,
        mesh=mesh,
        in_specs=placed,
        out_specs=(P(None, ("sites", "blk"), None, None, None), P("sites", None)),
        check_vma=False,
    )
```

```python
import functools
import math

import jax
import jax.numpy as jnp
import numpy as np
from jax import lax
from jax.experimental import pallas as pl
from jax.experimental.pallas import tpu as pltpu
from jax.sharding import PartitionSpec as P

BIN_LAG = 9
ONSET_BINS = 4
CAPACITY = 2
SAMPLES = 512
F32 = jnp.float32
BF16 = jnp.bfloat16


def phase_table(freqs, rows):
    turns = np.arange(ONSET_BINS)[:, None] * BIN_LAG * np.arange(freqs)[None, :] % SAMPLES
    angles = 2.0 * math.pi / SAMPLES * turns
    both = np.stack([np.cos(angles), np.sin(angles)])
    return np.repeat(both.reshape(2 * ONSET_BINS, freqs), rows, axis=0).astype(np.float32)


def column(row):
    n = row.shape[1]
    diag = lax.broadcasted_iota(jnp.int32, (n, n), 0) == lax.broadcasted_iota(jnp.int32, (n, n), 1)
    return jnp.sum(jnp.where(diag, jnp.broadcast_to(row, (n, n)), 0.0), axis=1, keepdims=True)


def kernel(
    dims,
    green_ref,
    slip_ref,
    onset_ref,
    helper_ref,
    rupture_ref,
    shift_ref,
    rate_ref,
    phase_ref,
    out_ref,
    power_ref,
    gat,
    rows_ref,
    acc,
    cos_ref,
    sin_ref,
    high,
    low,
    pw,
    local_sem,
    ring_s,
    ring_r,
    sib_s,
    sib_r,
    pw_s,
    pw_r,
):
    devices, batches, items, variations, rupts, comps, freqs = dims
    subs = green_ref.shape[0]
    half_rows = subs // 2
    chips = devices // 2
    me = lax.axis_index("blk")
    core = me % 2
    chip = me // 2
    folded = chips % 2 == 0

    def chip_at(pos):
        if not folded:
            return pos
        back = pos // (chips // 2)
        return (1 - back) * 2 * pos + back * (2 * (chips - 1 - pos) + 1)

    if folded:
        odd = chip % 2
        q = (1 - odd) * (chip // 2) + odd * (chips - 1 - chip // 2)
    else:
        q = chip
    right = chip_at((q + 1) % chips) * 2 + core
    left = chip_at((q + chips - 1) % chips) * 2 + core
    sibling = chip * 2 + (1 - core)

    def chunk(side, j, shift, which):
        step = j // 2 + shift
        pos = (q + chips - step) % chips if side == 0 else (q + step) % chips
        half = j % 2 if side == 0 else 1 - j % 2
        return gat.at[pos * 2 + which, pl.ds(pl.multiple_of(half * half_rows, half_rows), half_rows)]

    def ring(side, j, shift):
        piece = chunk(side, j, shift, core)
        return pltpu.make_async_remote_copy(
            src_ref=piece,
            dst_ref=piece,
            send_sem=ring_s.at[side, j],
            recv_sem=ring_r.at[side, j],
            device_id={"blk": right if side == 0 else left},
            device_id_type=pl.DeviceIdType.MESH,
        )

    def sib(side, j, which):
        piece = chunk(side, j, 1, which)
        return pltpu.make_async_remote_copy(
            src_ref=piece,
            dst_ref=piece,
            send_sem=sib_s.at[side, j],
            recv_sem=sib_r.at[side, j],
            device_id={"blk": sibling},
            device_id_type=pl.DeviceIdType.MESH,
        )

    def sib_own(half, which):
        piece = gat.at[q * 2 + which, pl.ds(half * half_rows, half_rows)]
        return pltpu.make_async_remote_copy(
            src_ref=piece,
            dst_ref=piece,
            send_sem=sib_s.at[half, chips - 1],
            recv_sem=sib_r.at[half, chips - 1],
            device_id={"blk": sibling},
            device_id_type=pl.DeviceIdType.MESH,
        )

    own = pltpu.make_async_copy(green_ref, gat.at[q * 2 + core], local_sem.at[0])
    own.start()
    barrier = pltpu.get_barrier_semaphore()

    for peer in (right, left, sibling):
        pl.semaphore_signal(barrier, inc=1, device_id={"blk": peer}, device_id_type=pl.DeviceIdType.MESH)

    pl.semaphore_wait(barrier, 3)
    own.wait()
    for j in range(min(2, chips - 1)):
        for side in range(2):
            ring(side, j, 0).start()
    for half in range(2):
        sib_own(half, core).start()

    total = batches * items
    lanes = total * variations
    slots = batches * CAPACITY
    group = ONSET_BINS * variations
    cols = subs
    helper_col = jnp.concatenate([column(helper_ref[b].astype(F32)) for b in range(batches)], axis=0)
    rupture_col = jnp.concatenate(
        [column(rupture_ref[b : b + 1, :].astype(F32)) for b in range(batches)], axis=0
    )
    lane = lax.broadcasted_iota(jnp.int32, (total, lanes), 1)
    lane_item = lane // variations
    item = lax.broadcasted_iota(jnp.int32, (total, lanes), 0)
    helper_lane = jnp.sum(jnp.where(lane_item == item, helper_col, 0.0), axis=0, keepdims=True)
    earlier = jnp.logical_and(item < lane_item, item // items == lane_item // items)
    same = jnp.logical_and(helper_col == helper_lane, earlier)
    rank = jnp.sum(jnp.where(same, 1.0, 0.0), axis=0, keepdims=True)
    lane1 = lax.broadcasted_iota(jnp.int32, (1, lanes), 1)
    batch1 = lane1 // (variations * items)
    key = (helper_lane.astype(jnp.int32) * slots + batch1 * CAPACITY + rank.astype(jnp.int32)) * variations
    key = key + lane1 % variations
    target = lax.broadcasted_iota(jnp.int32, (slots * group, lanes), 0)
    target = target // group * variations + target % variations
    slip_rows = slip_ref[...].astype(F32).reshape(lanes, subs)
    rows_ref[:, :cols] = slip_rows.astype(BF16)
    onset_rows = onset_ref[...].astype(F32).reshape(total, 1, subs)
    onset_rows = jnp.broadcast_to(onset_rows, (total, variations, subs)).reshape(lanes, subs)
    rows_ref[:, cols : 2 * cols] = onset_rows.astype(BF16)
    rupture_rows = jnp.broadcast_to(rupture_col, (total, 128)).reshape(total, 1, 128)
    rupture_rows = jnp.broadcast_to(rupture_rows, (total, variations, 128)).reshape(lanes, 128)
    rows_ref[:, 2 * cols :] = rupture_rows.astype(BF16)
    row_bin = lax.broadcasted_iota(jnp.int32, (slots * group, subs), 0) % group // variations
    row_bin = row_bin.astype(F32)
    acc[...] = jnp.zeros_like(acc)

    def compute(pos, which):
        h = chip_at(pos) * 2 + which
        pick = jnp.where(key - h * (slots * variations) == target, 1.0, 0.0).astype(BF16)
        picked = jnp.dot(pick, rows_ref[...], preferred_element_type=F32)
        masked = jnp.where(picked[:, cols : 2 * cols] == row_bin, picked[:, :cols], 0.0).astype(BF16)
        rupture = picked[:, 2 * cols :]
        for c in range(comps):
            lo = c * 2 * freqs
            summed = jnp.dot(
                masked, gat[pos * 2 + which, :, lo : lo + 2 * freqs], preferred_element_type=F32
            )
            for slot in range(slots):
                real_part = summed[slot * group : slot * group + variations, :freqs]
                imag_part = summed[slot * group : slot * group + variations, freqs:]
                real_sum, imag_sum = real_part, imag_part
                for k in range(1, ONSET_BINS):
                    at = slot * group + k * variations
                    real_part = summed[at : at + variations, :freqs]
                    imag_part = summed[at : at + variations, freqs:]
                    cos_k = phase_ref[k * variations : (k + 1) * variations, :]
                    s = (ONSET_BINS + k) * variations
                    sin_k = phase_ref[s : s + variations, :]
                    real_sum = real_sum + (cos_k * real_part + sin_k * imag_part)
                    imag_sum = imag_sum + (cos_k * imag_part - sin_k * real_part)
                both = jnp.concatenate([real_sum, imag_sum], axis=1).astype(BF16).astype(F32)
                named = rupture[slot * group : slot * group + variations, :]
                named = jnp.concatenate([named] * (2 * freqs // 128), axis=1)
                b = slot // CAPACITY
                for r in range(rupts):
                    base = (b * rupts + r) * variations
                    acc[base : base + variations, lo : lo + 2 * freqs] += jnp.where(
                        named == float(r), both, 0.0
                    )

    def arrive(j):
        for side in range(2):
            ring(side, j, 1).wait_recv()

            @pl.when(j + 2 <= chips - 2)
            def _():
                ring(side, j + 2, 0).start()

            sib(side, j, core).start()

    def sib_wait(j):
        for side in range(2):
            sib(side, j, 1 - core).wait_recv()

    def several(d, count):
        @pl.loop(0, count)
        def _(t):
            step = d - t // 2
            other = t // 2
            pos = (q + chips + (2 * (t % 2) - 1) * step) % chips
            compute(pos, core + other - 2 * core * other)

    frequency = lax.broadcasted_iota(jnp.int32, (variations, freqs), 1)
    for b in range(batches):
        for r in range(rupts):
            shift = column(shift_ref[b, r : r + 1, :].astype(F32)).astype(jnp.int32)
            turns = shift * frequency % SAMPLES
            angles = 2.0 * math.pi / SAMPLES * turns.astype(F32)
            base = (b * rupts + r) * variations
            cos_ref[base : base + variations, :] = jnp.cos(angles)
            sin_ref[base : base + variations, :] = jnp.sin(angles)

    compute(q, core)
    most = (chips - 1) // 2
    arrive(0)
    arrive(1)
    for half in range(2):
        sib_own(half, 1 - core).wait_recv()
    several(1, 3)

    strip = math.gcd(freqs, 32)

    @pl.loop(0, freqs // strip)
    def _(i):
        first = pl.multiple_of(i * strip, strip)
        f = lax.broadcasted_iota(jnp.int32, (strip, SAMPLES), 0) + first
        turns = f * lax.broadcasted_iota(jnp.int32, (strip, SAMPLES), 1) % SAMPLES
        angles = 2.0 * math.pi / SAMPLES * turns.astype(F32)
        weight = jnp.where(f == 0, 1.0 / SAMPLES, 2.0 / SAMPLES)
        for values, base in ((weight * jnp.cos(angles), 0), (-weight * jnp.sin(angles), freqs)):
            rounded = values.astype(BF16)
            at = pl.ds(pl.multiple_of(base + first, strip), strip)
            high[at, :] = rounded
            low[at, :] = (values - rounded.astype(F32)).astype(BF16)

    @pl.loop(2, most + 1)
    def _(d):
        arrive(2 * d - 2)
        arrive(2 * d - 1)
        sib_wait(2 * d - 4)
        sib_wait(2 * d - 3)
        several(d, 4)

    sib_wait(2 * most - 2)
    sib_wait(2 * most - 1)
    compute((q + chips - most) % chips, 1 - core)
    compute((q + most) % chips, 1 - core)
    if folded:
        arrive(chips - 2)
        compute((q + chips // 2) % chips, core)
        sib_wait(chips - 2)
        compute((q + chips // 2) % chips, 1 - core)

    for c in range(comps):
        lo = c * 2 * freqs
        energy = jnp.zeros((variations, freqs), F32)
        for b in range(batches):
            for r in range(rupts):
                base = (b * rupts + r) * variations
                real_part = acc[base : base + variations, lo : lo + freqs]
                imag_part = acc[base : base + variations, lo + freqs : lo + 2 * freqs]
                square = real_part * real_part + imag_part * imag_part
                energy = energy + rate_ref[b : b + 1, r : r + 1] * square
        pw[me, c : c + 1, :] = jnp.sum(energy, axis=0, keepdims=True) * (1.0 / variations)

    def power_copy(o):
        return pltpu.make_async_remote_copy(
            src_ref=pw.at[me],
            dst_ref=pw.at[me],
            send_sem=pw_s.at[o],
            recv_sem=pw_r.at[o],
            device_id={"blk": (me + o) % devices},
            device_id_type=pl.DeviceIdType.MESH,
        )

    def power_arrival(o):
        slot = pw.at[(me + devices - o) % devices]
        return pltpu.make_async_remote_copy(
            src_ref=slot,
            dst_ref=slot,
            send_sem=pw_s.at[o],
            recv_sem=pw_r.at[o],
            device_id={"blk": (me + o) % devices},
            device_id_type=pl.DeviceIdType.MESH,
        )

    @pl.loop(1, devices)
    def _(o):
        power_copy(o).start()

    cos_shift = cos_ref[...]
    sin_shift = sin_ref[...]
    shifted = []
    for c in range(comps):
        lo = c * 2 * freqs
        real_part = acc[:, lo : lo + freqs]
        imag_part = acc[:, lo + freqs : lo + 2 * freqs]
        shifted.append(
            jnp.concatenate(
                [
                    real_part * cos_shift + imag_part * sin_shift,
                    imag_part * cos_shift - real_part * sin_shift,
                ],
                axis=1,
            )
        )
    shifted = jnp.concatenate(shifted, axis=0)
    shifted_high = shifted.astype(BF16)
    shifted_low = (shifted - shifted_high.astype(F32)).astype(BF16)
    seismo = jnp.dot(shifted_high, high[...], preferred_element_type=F32)
    seismo = seismo + jnp.dot(shifted_low, high[...], preferred_element_type=F32)
    seismo = seismo + jnp.dot(shifted_high, low[...], preferred_element_type=F32)
    count = acc.shape[0]
    for c in range(comps):
        out_ref[:, c * SAMPLES : (c + 1) * SAMPLES] = seismo[c * count : (c + 1) * count, :]

    @pl.loop(1, devices)
    def _(o):
        power_arrival(o).wait_recv()

    power_ref[...] = jnp.log(jnp.sum(pw[...], axis=0))

    @pl.loop(1, devices)
    def _(o):
        power_copy(o).wait_send()

    @pl.loop(0, chips - 1)
    def _(j):
        for side in range(2):
            ring(side, j, 0).wait_send()
            sib(side, j, core).wait_send()

    for half in range(2):
        sib_own(half, core).wait_send()


def local(green, slip, onset_bin, item_helper, item_rupture, base_shift, rupture_rate):
    devices = lax.axis_size("blk")
    subs, comps, _, freqs = green.shape
    batches, items, variations, _ = slip.shape
    rupts = base_shift.shape[1]
    width = comps * 2 * freqs
    rows = batches * rupts * variations
    chips = devices // 2
    dims = (devices, batches, items, variations, rupts, comps, freqs)
    gathered = devices * subs * width * 2
    vmem = pl.BlockSpec(memory_space=pltpu.VMEM)
    anywhere = pl.BlockSpec(memory_space=pl.ANY)
    seismo, power = pl.pallas_call(
        functools.partial(kernel, dims),
        out_shape=(
            jax.ShapeDtypeStruct((rows, comps * SAMPLES), F32),
            jax.ShapeDtypeStruct((comps, freqs), F32),
        ),
        in_specs=[anywhere, vmem, vmem, vmem, vmem, vmem, vmem, vmem],
        out_specs=(vmem, vmem),
        scratch_shapes=[
            pltpu.VMEM((devices, subs, width), BF16),
            pltpu.VMEM((batches * items * variations, 2 * subs + 128), BF16),
            pltpu.VMEM((rows, width), F32),
            pltpu.VMEM((rows, freqs), F32),
            pltpu.VMEM((rows, freqs), F32),
            pltpu.VMEM((2 * freqs, SAMPLES), BF16),
            pltpu.VMEM((2 * freqs, SAMPLES), BF16),
            pltpu.VMEM((devices, comps, freqs), F32),
            pltpu.SemaphoreType.DMA((1,)),
            pltpu.SemaphoreType.DMA((2, chips)),
            pltpu.SemaphoreType.DMA((2, chips)),
            pltpu.SemaphoreType.DMA((2, chips)),
            pltpu.SemaphoreType.DMA((2, chips)),
            pltpu.SemaphoreType.DMA((devices,)),
            pltpu.SemaphoreType.DMA((devices,)),
        ],
        compiler_params=pltpu.CompilerParams(
            collective_id=0, has_side_effects=True, vmem_limit_bytes=min(60, 20 + (gathered >> 20)) << 20
        ),
    )(
        green.reshape(subs, width),
        slip,
        onset_bin,
        item_helper.reshape(batches, 1, items),
        item_rupture,
        base_shift,
        rupture_rate,
        jnp.asarray(phase_table(freqs, variations)),
    )
    return seismo.reshape(batches, rupts, variations, comps, SAMPLES), power


def solution(mesh):
    placed = (
        P(("sites", "blk"), None, None, None),
        P(None, "blk", None, None),
        P(None, "blk", None),
        P(None, "blk", None),
        P(None, "blk"),
        P(None, "blk", None),
        P(None, "blk"),
    )
    return jax.shard_map(
        local,
        mesh=mesh,
        in_specs=placed,
        out_specs=(P(None, ("sites", "blk"), None, None, None), P("sites", None)),
        check_vma=False,
    )
```

```python
import functools
import math

import jax
import jax.numpy as jnp
import numpy as np
from jax import lax
from jax.experimental import pallas as pl
from jax.experimental.pallas import tpu as pltpu
from jax.sharding import PartitionSpec as P

BIN_LAG = 9
ONSET_BINS = 4
CAPACITY = 2
SAMPLES = 512
F32 = jnp.float32
BF16 = jnp.bfloat16


def phase_table(freqs, rows):
    turns = np.arange(ONSET_BINS)[:, None] * BIN_LAG * np.arange(freqs)[None, :] % SAMPLES
    angles = 2.0 * math.pi / SAMPLES * turns
    both = np.stack([np.cos(angles), np.sin(angles)])
    return np.repeat(both.reshape(2 * ONSET_BINS, freqs), rows, axis=0).astype(np.float32)


def column(row):
    n = row.shape[1]
    diag = lax.broadcasted_iota(jnp.int32, (n, n), 0) == lax.broadcasted_iota(jnp.int32, (n, n), 1)
    return jnp.sum(jnp.where(diag, jnp.broadcast_to(row, (n, n)), 0.0), axis=1, keepdims=True)


def kernel(
    dims,
    green_ref,
    slip_ref,
    onset_ref,
    helper_ref,
    rupture_ref,
    shift_ref,
    rate_ref,
    phase_ref,
    out_ref,
    power_ref,
    gat,
    rows_ref,
    acc,
    cos_ref,
    sin_ref,
    high,
    low,
    pw,
    local_sem,
    ring_s,
    ring_r,
    sib_s,
    sib_r,
    pw_s,
    pw_r,
):
    devices, batches, items, variations, rupts, comps, freqs = dims
    subs = green_ref.shape[0]
    half_rows = subs // 2
    chips = devices // 2
    me = lax.axis_index("blk")
    core = me % 2
    chip = me // 2
    folded = chips % 2 == 0

    def chip_at(pos):
        if not folded:
            return pos
        back = pos // (chips // 2)
        return (1 - back) * 2 * pos + back * (2 * (chips - 1 - pos) + 1)

    if folded:
        odd = chip % 2
        q = (1 - odd) * (chip // 2) + odd * (chips - 1 - chip // 2)
    else:
        q = chip
    right = chip_at((q + 1) % chips) * 2 + core
    left = chip_at((q + chips - 1) % chips) * 2 + core
    sibling = chip * 2 + (1 - core)

    def chunk(side, j, shift, which):
        step = j // 2 + shift
        pos = (q + chips - step) % chips if side == 0 else (q + step) % chips
        half = j % 2 if side == 0 else 1 - j % 2
        return gat.at[pos * 2 + which, pl.ds(pl.multiple_of(half * half_rows, half_rows), half_rows)]

    def ring(side, j, shift):
        piece = chunk(side, j, shift, core)
        return pltpu.make_async_remote_copy(
            src_ref=piece,
            dst_ref=piece,
            send_sem=ring_s.at[side, j],
            recv_sem=ring_r.at[side, j],
            device_id={"blk": right if side == 0 else left},
            device_id_type=pl.DeviceIdType.MESH,
        )

    def sib(side, j, which):
        piece = chunk(side, j, 1, which)
        return pltpu.make_async_remote_copy(
            src_ref=piece,
            dst_ref=piece,
            send_sem=sib_s.at[side, j],
            recv_sem=sib_r.at[side, j],
            device_id={"blk": sibling},
            device_id_type=pl.DeviceIdType.MESH,
        )

    def sib_own(half, which):
        piece = gat.at[q * 2 + which, pl.ds(half * half_rows, half_rows)]
        return pltpu.make_async_remote_copy(
            src_ref=piece,
            dst_ref=piece,
            send_sem=sib_s.at[half, chips - 1],
            recv_sem=sib_r.at[half, chips - 1],
            device_id={"blk": sibling},
            device_id_type=pl.DeviceIdType.MESH,
        )

    own = pltpu.make_async_copy(green_ref, gat.at[q * 2 + core], local_sem.at[0])
    own.start()
    barrier = pltpu.get_barrier_semaphore()

    for peer in (right, left, sibling):
        pl.semaphore_signal(barrier, inc=1, device_id={"blk": peer}, device_id_type=pl.DeviceIdType.MESH)

    pl.semaphore_wait(barrier, 3)
    own.wait()
    for j in range(min(2, chips - 1)):
        for side in range(2):
            ring(side, j, 0).start()
    for half in range(2):
        sib_own(half, core).start()

    total = batches * items
    lanes = total * variations
    slots = batches * CAPACITY
    group = ONSET_BINS * variations
    cols = subs
    helper_col = jnp.concatenate([column(helper_ref[b].astype(F32)) for b in range(batches)], axis=0)
    rupture_col = jnp.concatenate(
        [column(rupture_ref[b : b + 1, :].astype(F32)) for b in range(batches)], axis=0
    )
    lane = lax.broadcasted_iota(jnp.int32, (total, lanes), 1)
    lane_item = lane // variations
    item = lax.broadcasted_iota(jnp.int32, (total, lanes), 0)
    helper_lane = jnp.sum(jnp.where(lane_item == item, helper_col, 0.0), axis=0, keepdims=True)
    earlier = jnp.logical_and(item < lane_item, item // items == lane_item // items)
    same = jnp.logical_and(helper_col == helper_lane, earlier)
    rank = jnp.sum(jnp.where(same, 1.0, 0.0), axis=0, keepdims=True)
    lane1 = lax.broadcasted_iota(jnp.int32, (1, lanes), 1)
    batch1 = lane1 // (variations * items)
    key = (helper_lane.astype(jnp.int32) * slots + batch1 * CAPACITY + rank.astype(jnp.int32)) * variations
    key = key + lane1 % variations
    target = lax.broadcasted_iota(jnp.int32, (slots * group, lanes), 0)
    target = target // group * variations + target % variations
    slip_rows = slip_ref[...].astype(F32).reshape(lanes, subs)
    rows_ref[:, :cols] = slip_rows.astype(BF16)
    onset_rows = onset_ref[...].astype(F32).reshape(total, 1, subs)
    onset_rows = jnp.broadcast_to(onset_rows, (total, variations, subs)).reshape(lanes, subs)
    rows_ref[:, cols : 2 * cols] = onset_rows.astype(BF16)
    rupture_rows = jnp.broadcast_to(rupture_col, (total, 128)).reshape(total, 1, 128)
    rupture_rows = jnp.broadcast_to(rupture_rows, (total, variations, 128)).reshape(lanes, 128)
    rows_ref[:, 2 * cols :] = rupture_rows.astype(BF16)
    row_bin = lax.broadcasted_iota(jnp.int32, (slots * group, subs), 0) % group // variations
    row_bin = row_bin.astype(F32)
    acc[...] = jnp.zeros_like(acc)

    def prepare(pos, which):
        h = chip_at(pos) * 2 + which
        pick = jnp.where(key - h * (slots * variations) == target, 1.0, 0.0).astype(BF16)
        picked = jnp.dot(pick, rows_ref[...], preferred_element_type=F32)
        masked = jnp.where(picked[:, cols : 2 * cols] == row_bin, picked[:, :cols], 0.0).astype(BF16)
        return masked, picked[:, 2 * cols :]

    def finish(pos, which, prepared):
        masked, rupture = prepared
        for c in range(comps):
            lo = c * 2 * freqs
            summed = jnp.dot(
                masked, gat[pos * 2 + which, :, lo : lo + 2 * freqs], preferred_element_type=F32
            )
            for slot in range(slots):
                real_part = summed[slot * group : slot * group + variations, :freqs]
                imag_part = summed[slot * group : slot * group + variations, freqs:]
                real_sum, imag_sum = real_part, imag_part
                for k in range(1, ONSET_BINS):
                    at = slot * group + k * variations
                    real_part = summed[at : at + variations, :freqs]
                    imag_part = summed[at : at + variations, freqs:]
                    cos_k = phase_ref[k * variations : (k + 1) * variations, :]
                    s = (ONSET_BINS + k) * variations
                    sin_k = phase_ref[s : s + variations, :]
                    real_sum = real_sum + (cos_k * real_part + sin_k * imag_part)
                    imag_sum = imag_sum + (cos_k * imag_part - sin_k * real_part)
                both = jnp.concatenate([real_sum, imag_sum], axis=1).astype(BF16).astype(F32)
                named = rupture[slot * group : slot * group + variations, :]
                named = jnp.concatenate([named] * (2 * freqs // 128), axis=1)
                b = slot // CAPACITY
                for r in range(rupts):
                    base = (b * rupts + r) * variations
                    acc[base : base + variations, lo : lo + 2 * freqs] += jnp.where(
                        named == float(r), both, 0.0
                    )

    def compute(pos, which):
        finish(pos, which, prepare(pos, which))

    def arrive(j):
        for side in range(2):
            ring(side, j, 1).wait_recv()

            @pl.when(j + 2 <= chips - 2)
            def _():
                ring(side, j + 2, 0).start()

            sib(side, j, core).start()

    def sib_wait(j):
        for side in range(2):
            sib(side, j, 1 - core).wait_recv()

    def several(d, count):
        @pl.loop(0, count)
        def _(t):
            step = d - t // 2
            other = t // 2
            pos = (q + chips + (2 * (t % 2) - 1) * step) % chips
            compute(pos, core + other - 2 * core * other)

    frequency = lax.broadcasted_iota(jnp.int32, (variations, freqs), 1)
    for b in range(batches):
        for r in range(rupts):
            shift = column(shift_ref[b, r : r + 1, :].astype(F32)).astype(jnp.int32)
            turns = shift * frequency % SAMPLES
            angles = 2.0 * math.pi / SAMPLES * turns.astype(F32)
            base = (b * rupts + r) * variations
            cos_ref[base : base + variations, :] = jnp.cos(angles)
            sin_ref[base : base + variations, :] = jnp.sin(angles)

    compute(q, core)
    most = (chips - 1) // 2
    arrive(0)
    arrive(1)
    for half in range(2):
        sib_own(half, 1 - core).wait_recv()
    several(1, 3)

    strip = math.gcd(freqs, 32)

    @pl.loop(0, freqs // strip)
    def _(i):
        first = pl.multiple_of(i * strip, strip)
        f = lax.broadcasted_iota(jnp.int32, (strip, SAMPLES), 0) + first
        turns = f * lax.broadcasted_iota(jnp.int32, (strip, SAMPLES), 1) % SAMPLES
        angles = 2.0 * math.pi / SAMPLES * turns.astype(F32)
        weight = jnp.where(f == 0, 1.0 / SAMPLES, 2.0 / SAMPLES)
        for values, base in ((weight * jnp.cos(angles), 0), (-weight * jnp.sin(angles), freqs)):
            rounded = values.astype(BF16)
            at = pl.ds(pl.multiple_of(base + first, strip), strip)
            high[at, :] = rounded
            low[at, :] = (values - rounded.astype(F32)).astype(BF16)

    @pl.loop(2, most + 1)
    def _(d):
        arrive(2 * d - 2)
        arrive(2 * d - 1)
        sib_wait(2 * d - 4)
        sib_wait(2 * d - 3)
        several(d, 4)

    sib_wait(2 * most - 2)
    sib_wait(2 * most - 1)
    compute((q + chips - most) % chips, 1 - core)
    compute((q + most) % chips, 1 - core)
    if folded:
        across = (q + chips // 2) % chips
        first, second = prepare(across, core), prepare(across, 1 - core)
        arrive(chips - 2)
        finish(across, core, first)
        sib_wait(chips - 2)
        finish(across, 1 - core, second)

    for c in range(comps):
        lo = c * 2 * freqs
        energy = jnp.zeros((variations, freqs), F32)
        for b in range(batches):
            for r in range(rupts):
                base = (b * rupts + r) * variations
                real_part = acc[base : base + variations, lo : lo + freqs]
                imag_part = acc[base : base + variations, lo + freqs : lo + 2 * freqs]
                square = real_part * real_part + imag_part * imag_part
                energy = energy + rate_ref[b : b + 1, r : r + 1] * square
        pw[me, c : c + 1, :] = jnp.sum(energy, axis=0, keepdims=True) * (1.0 / variations)

    def power_copy(o):
        return pltpu.make_async_remote_copy(
            src_ref=pw.at[me],
            dst_ref=pw.at[me],
            send_sem=pw_s.at[o],
            recv_sem=pw_r.at[o],
            device_id={"blk": lax.rem(me + o, devices)},
            device_id_type=pl.DeviceIdType.MESH,
        )

    def power_arrival(o):
        slot = pw.at[lax.rem(me + devices - o, devices)]
        return pltpu.make_async_remote_copy(
            src_ref=slot,
            dst_ref=slot,
            send_sem=pw_s.at[o],
            recv_sem=pw_r.at[o],
            device_id={"blk": lax.rem(me + o, devices)},
            device_id_type=pl.DeviceIdType.MESH,
        )

    @pl.loop(1, devices, unroll=math.gcd(devices - 1, 5))
    def _(o):
        power_copy(o).start()

    cos_shift = cos_ref[...]
    sin_shift = sin_ref[...]
    shifted = []
    for c in range(comps):
        lo = c * 2 * freqs
        real_part = acc[:, lo : lo + freqs]
        imag_part = acc[:, lo + freqs : lo + 2 * freqs]
        shifted.append(
            jnp.concatenate(
                [
                    real_part * cos_shift + imag_part * sin_shift,
                    imag_part * cos_shift - real_part * sin_shift,
                ],
                axis=1,
            )
        )
    shifted = jnp.concatenate(shifted, axis=0)
    shifted_high = shifted.astype(BF16)
    shifted_low = (shifted - shifted_high.astype(F32)).astype(BF16)
    seismo = jnp.dot(shifted_high, high[...], preferred_element_type=F32)
    seismo = seismo + jnp.dot(shifted_low, high[...], preferred_element_type=F32)
    seismo = seismo + jnp.dot(shifted_high, low[...], preferred_element_type=F32)
    count = acc.shape[0]
    for c in range(comps):
        out_ref[:, c * SAMPLES : (c + 1) * SAMPLES] = seismo[c * count : (c + 1) * count, :]

    @pl.loop(1, devices, unroll=math.gcd(devices - 1, 5))
    def _(o):
        power_arrival(o).wait_recv()

    power_ref[...] = jnp.log(jnp.sum(pw[...], axis=0))

    @pl.loop(1, devices, unroll=math.gcd(devices - 1, 5))
    def _(o):
        power_copy(o).wait_send()

    @pl.loop(0, chips - 1)
    def _(j):
        for side in range(2):
            ring(side, j, 0).wait_send()
            sib(side, j, core).wait_send()

    for half in range(2):
        sib_own(half, core).wait_send()


def local(green, slip, onset_bin, item_helper, item_rupture, base_shift, rupture_rate):
    devices = lax.axis_size("blk")
    subs, comps, _, freqs = green.shape
    batches, items, variations, _ = slip.shape
    rupts = base_shift.shape[1]
    width = comps * 2 * freqs
    rows = batches * rupts * variations
    chips = devices // 2
    dims = (devices, batches, items, variations, rupts, comps, freqs)
    gathered = devices * subs * width * 2
    vmem = pl.BlockSpec(memory_space=pltpu.VMEM)
    anywhere = pl.BlockSpec(memory_space=pl.ANY)
    seismo, power = pl.pallas_call(
        functools.partial(kernel, dims),
        out_shape=(
            jax.ShapeDtypeStruct((rows, comps * SAMPLES), F32),
            jax.ShapeDtypeStruct((comps, freqs), F32),
        ),
        in_specs=[anywhere, vmem, vmem, vmem, vmem, vmem, vmem, vmem],
        out_specs=(vmem, vmem),
        scratch_shapes=[
            pltpu.VMEM((devices, subs, width), BF16),
            pltpu.VMEM((batches * items * variations, 2 * subs + 128), BF16),
            pltpu.VMEM((rows, width), F32),
            pltpu.VMEM((rows, freqs), F32),
            pltpu.VMEM((rows, freqs), F32),
            pltpu.VMEM((2 * freqs, SAMPLES), BF16),
            pltpu.VMEM((2 * freqs, SAMPLES), BF16),
            pltpu.VMEM((devices, comps, freqs), F32),
            pltpu.SemaphoreType.DMA((1,)),
            pltpu.SemaphoreType.DMA((2, chips)),
            pltpu.SemaphoreType.DMA((2, chips)),
            pltpu.SemaphoreType.DMA((2, chips)),
            pltpu.SemaphoreType.DMA((2, chips)),
            pltpu.SemaphoreType.DMA((devices,)),
            pltpu.SemaphoreType.DMA((devices,)),
        ],
        compiler_params=pltpu.CompilerParams(
            collective_id=0, has_side_effects=True, vmem_limit_bytes=min(60, 20 + (gathered >> 20)) << 20
        ),
    )(
        green.reshape(subs, width),
        slip,
        onset_bin,
        item_helper.reshape(batches, 1, items),
        item_rupture,
        base_shift,
        rupture_rate,
        jnp.asarray(phase_table(freqs, variations)),
    )
    return seismo.reshape(batches, rupts, variations, comps, SAMPLES), power


def solution(mesh):
    placed = (
        P(("sites", "blk"), None, None, None),
        P(None, "blk", None, None),
        P(None, "blk", None),
        P(None, "blk", None),
        P(None, "blk"),
        P(None, "blk", None),
        P(None, "blk"),
    )
    return jax.shard_map(
        local,
        mesh=mesh,
        in_specs=placed,
        out_specs=(P(None, ("sites", "blk"), None, None, None), P("sites", None)),
        check_vma=False,
    )
```
